128 devices in a mesh: dp: 16 (over z_hi, y, core), tensor: 8 (over x, z_lo).
Axes of the slice: x: 4, y: 4, z: 4 (z_hi: 2, z_lo: 2; z = z_hi * 2 + z_lo), core: 2. Of those that a mesh axis runs over, the one named last changes fastest.
Arguments:
- tokens: bfloat16 [16384, 1024], P(('dp', 'tensor')), may hold values from -6 to 6
- out_grad: bfloat16 [16384, 1024], P(('dp', 'tensor')), may hold values from -6 to 6
- lengths: int32 [16, 4], P('dp'), may hold values from 0 to 1024, as said below
- w_query: float32 [1024, 2048], P('dp', 'tensor'), may hold values from -0.1875 to 0.1875
- key_weight: float32 [1024, 1024], P('dp', 'tensor'), may hold values from -0.1875 to 0.1875
- value_weight: float32 [1024, 1024], P('dp', 'tensor'), may hold values from -0.1875 to 0.1875
- w_output: float32 [2048, 1024], P('tensor', 'dp'), may hold values from -0.5 to 0.5
- w_gate: float32 [1024, 3072], P('dp', 'tensor'), may hold values from -0.1875 to 0.1875
- w_up: float32 [1024, 3072], P('dp', 'tensor'), may hold values from -0.1875 to 0.1875
- w_down: float32 [3072, 1024], P('tensor', 'dp'), may hold values from -0.109375 to 0.109375
- momentum_query: float32 [1024, 2048], P('dp', 'tensor'), may hold values from -224 to 224
- key_momentum_buffer: float32 [1024, 1024], P('dp', 'tensor'), may hold values from -224 to 224
- value_momentum_buffer: float32 [1024, 1024], P('dp', 'tensor'), may hold values from -768 to 768
- momentum_output: float32 [2048, 1024], P('tensor', 'dp'), may hold values from -160 to 160
- momentum_gate: float32 [1024, 3072], P('dp', 'tensor'), may hold values from -224 to 224
- momentum_up: float32 [1024, 3072], P('dp', 'tensor'), may hold values from -224 to 224
- momentum_down: float32 [3072, 1024], P('tensor', 'dp'), may hold values from -448 to 448
- gains: float32 [2304], replicated, may hold values from 0.5 to 1.5
- gain_first: float32 [2304], replicated, may hold values from -32 to 32
- gain_second: float32 [2304], replicated, may hold values from 137.6256 to 557.056
Outputs:
- out: bfloat16 [16384, 1024], P(('dp', 'tensor'))
- tokens_grad: float32 [16384, 1024], P(('dp', 'tensor'))
- grad_query: float32 [1024, 2048], P('dp', 'tensor')
- grad_key: float32 [1024, 1024], P('dp', 'tensor')
- grad_value: float32 [1024, 1024], P('dp', 'tensor')
- grad_output: float32 [2048, 1024], P('tensor', 'dp')
- grad_gate: float32 [1024, 3072], P('dp', 'tensor')
- grad_up: float32 [1024, 3072], P('dp', 'tensor')
- grad_down: float32 [3072, 1024], P('tensor', 'dp')
- renewed_query: float32 [1024, 2048], P('dp', 'tensor')
- renewed_key: float32 [1024, 1024], P('dp', 'tensor')
- renewed_value: float32 [1024, 1024], P('dp', 'tensor')
- renewed_output: float32 [2048, 1024], P('tensor', 'dp')
- renewed_gate: float32 [1024, 3072], P('dp', 'tensor')
- renewed_up: float32 [1024, 3072], P('dp', 'tensor')
- renewed_down: float32 [3072, 1024], P('tensor', 'dp')
- updated_query: float32 [1024, 2048], P('dp', 'tensor')
- updated_key: float32 [1024, 1024], P('dp', 'tensor')
- updated_value: float32 [1024, 1024], P('dp', 'tensor')
- updated_output: float32 [2048, 1024], P('tensor', 'dp')
- updated_gate: float32 [1024, 3072], P('dp', 'tensor')
- updated_up: float32 [1024, 3072], P('dp', 'tensor')
- updated_down: float32 [3072, 1024], P('tensor', 'dp')
- gain_grad: float32 [2304], replicated
- renewed_first: float32 [2304], replicated
- renewed_second: float32 [2304], replicated
- updated_gains: float32 [2304], replicated
The draws below stay inside these ranges and needn't reach their ends.
Inputs may be any that keep to these rules, and one draw needn't show every extreme that they name: In each group the 4 lengths sum to 1024; some lengths may be zero.
All inputs are finite; a program needn't handle non-finite values.
Results may differ from the reference program's by a relative error of at most 0.013.
The reference program's roundings to bfloat16 on the way count: a program that leaves them out, or rounds other values in their place, can miss the bound.
Values may be sent and summed in bfloat16 or wider, within the bound.
No kernel may reach another device: no remote copies, remote signals or barrier semaphores. Data moves between devices by JAX's collectives and lax.ppermute only.
A program may use at most 128 MiB of HBM per device.

```python
import math
import jax
import jax.numpy as jnp
from jax import lax

MODEL_WIDTH = 1024
QUERY_HEADS = 16
KEY_VALUE_HEADS = 8
HEAD_SIZE = 128
FF = 3072
TOK_DEV = 128
SLOTS = 4
NS_ITERS = 5
ADAM_STEP = 10
GROUP_ROWS = 1024
DP_GROUPS = 16
TOKEN_TOTAL = 16384
N_TENSOR = 8


def draw_lengths(key, part):
    key = jax.random.fold_in(key, 11)
    key_rest, key_full, key_cuts, key_slot = jax.random.split(key, 4)
    leftover = jax.random.randint(key_rest, (DP_GROUPS,), 0, TOK_DEV)
    full_group = jax.random.randint(key_full, (), 0, DP_GROUPS)
    leftover = jnp.where(jnp.arange(DP_GROUPS) == full_group, 0, leftover).astype(jnp.int32)
    cuts = jax.random.randint(key_cuts, (DP_GROUPS, SLOTS - 2), 0, leftover[:, None] + 1)
    cuts = jnp.sort(cuts, axis=1).astype(jnp.int32)
    edges = jnp.concatenate([jnp.zeros((DP_GROUPS, 1), jnp.int32), cuts, leftover[:, None]], axis=1)
    small_parts = edges[:, 1:] - edges[:, :-1]
    longest = GROUP_ROWS - leftover
    slot_of_long = jax.random.randint(key_slot, (DP_GROUPS,), 0, SLOTS)
    column = jnp.arange(SLOTS, dtype=jnp.int32)[None, :]
    empty_col = jnp.zeros((DP_GROUPS, 1), jnp.int32)
    before = jnp.concatenate([small_parts, empty_col], axis=1)
    after = jnp.concatenate([empty_col, small_parts], axis=1)
    chosen = jnp.where(column < slot_of_long[:, None], before, jnp.where(column == slot_of_long[:, None], longest[:, None], after))
    return chosen.astype(jnp.int32)


def steps_of(key, shape, shards, smallest, largest):
    loudness = 1.0
    for position, shards_of in shards:
        heights = jax.random.uniform(jax.random.fold_in(jax.random.fold_in(key, 6), position), (shards_of,), jnp.float32, smallest / len(shards), largest / len(shards))
        loudness = loudness * jnp.repeat(jnp.exp(heights), shape[position] // shards_of).reshape((-1,) + (1,) * (len(shape) - 1 - position))
    return loudness


def bell_draw(key, extent, scale, limit, cuts=(), kind=jnp.bfloat16):
    loudness = steps_of(key, extent, cuts, -0.22, 0.18) if cuts else 1.0
    drawn = jax.random.normal(key, extent, jnp.float32) * scale * loudness
    return jnp.minimum(jnp.maximum(drawn, -limit), limit).astype(kind)


def setup_inputs(seed: int = 0) -> dict:
    splits = jax.random.split(jax.random.key(seed), 21)
    tokens = bell_draw(splits[0], (TOKEN_TOTAL, MODEL_WIDTH), 1.0, 6.0, ((0, 128),))
    out_grad = bell_draw(splits[1], (TOKEN_TOTAL, MODEL_WIDTH), 1.0, 6.0, ((0, 128),))
    lengths = draw_lengths(jax.random.fold_in(splits[20], 71), 0)
    w_query = bell_draw(splits[3], (MODEL_WIDTH, QUERY_HEADS * HEAD_SIZE), MODEL_WIDTH ** -0.5, 0.1875, ((0, 16), (1, 8)), jnp.float32)
    key_weight = bell_draw(splits[4], (MODEL_WIDTH, KEY_VALUE_HEADS * HEAD_SIZE), MODEL_WIDTH ** -0.5, 0.1875, ((0, 16), (1, 8)), jnp.float32)
    value_weight = bell_draw(splits[5], (MODEL_WIDTH, KEY_VALUE_HEADS * HEAD_SIZE), MODEL_WIDTH ** -0.5, 0.1875, ((0, 16), (1, 8)), jnp.float32)
    w_output = bell_draw(splits[6], (QUERY_HEADS * HEAD_SIZE, MODEL_WIDTH), (QUERY_HEADS * HEAD_SIZE // 16) ** -0.5, 0.5, ((0, 8), (1, 16)), jnp.float32)
    w_gate = bell_draw(splits[7], (MODEL_WIDTH, FF), MODEL_WIDTH ** -0.5, 0.1875, ((0, 16), (1, 8)), jnp.float32)
    w_up = bell_draw(splits[8], (MODEL_WIDTH, FF), MODEL_WIDTH ** -0.5, 0.1875, ((0, 16), (1, 8)), jnp.float32)
    w_down = bell_draw(splits[9], (FF, MODEL_WIDTH), FF ** -0.5, 0.109375, ((0, 8), (1, 16)), jnp.float32)
    momentum_query = bell_draw(splits[10], (MODEL_WIDTH, QUERY_HEADS * HEAD_SIZE), (0.3 * TOKEN_TOTAL ** 0.5), 224.0, ((0, 16), (1, 8)), jnp.float32)
    key_momentum_buffer = bell_draw(splits[11], (MODEL_WIDTH, KEY_VALUE_HEADS * HEAD_SIZE), (0.3 * TOKEN_TOTAL ** 0.5), 224.0, ((0, 16), (1, 8)), jnp.float32)
    value_momentum_buffer = bell_draw(splits[12], (MODEL_WIDTH, KEY_VALUE_HEADS * HEAD_SIZE), (1.0 * TOKEN_TOTAL ** 0.5), 768.0, ((0, 16), (1, 8)), jnp.float32)
    momentum_output = bell_draw(splits[13], (QUERY_HEADS * HEAD_SIZE, MODEL_WIDTH), (0.2 * TOKEN_TOTAL ** 0.5), 160.0, ((0, 8), (1, 16)), jnp.float32)
    momentum_gate = bell_draw(splits[14], (MODEL_WIDTH, FF), (0.3 * TOKEN_TOTAL ** 0.5), 224.0, ((0, 16), (1, 8)), jnp.float32)
    momentum_up = bell_draw(splits[15], (MODEL_WIDTH, FF), (0.3 * TOKEN_TOTAL ** 0.5), 224.0, ((0, 16), (1, 8)), jnp.float32)
    momentum_down = bell_draw(splits[16], (FF, MODEL_WIDTH), (0.6 * TOKEN_TOTAL ** 0.5), 448.0, ((0, 8), (1, 16)), jnp.float32)
    gains = jnp.clip(1.0 + 0.1 * jax.random.normal(splits[17], (2 * MODEL_WIDTH + 2 * HEAD_SIZE,), jnp.float32), 0.5, 1.5)
    gain_first = bell_draw(splits[18], (2 * MODEL_WIDTH + 2 * HEAD_SIZE,), (0.04 * TOKEN_TOTAL ** 0.5), 32.0, (), jnp.float32)
    gain_second = jnp.clip(jnp.exp(jax.random.uniform(splits[19], (2 * MODEL_WIDTH + 2 * HEAD_SIZE,), jnp.float32, math.log(137.6256), math.log(557.056))), 137.6256, 557.056)
    return {"tokens": tokens, "out_grad": out_grad, "lengths": lengths, "w_query": w_query, "key_weight": key_weight, "value_weight": value_weight, "w_output": w_output, "w_gate": w_gate, "w_up": w_up, "w_down": w_down, "momentum_query": momentum_query, "key_momentum_buffer": key_momentum_buffer, "value_momentum_buffer": value_momentum_buffer, "momentum_output": momentum_output, "momentum_gate": momentum_gate, "momentum_up": momentum_up, "momentum_down": momentum_down, "gains": gains, "gain_first": gain_first, "gain_second": gain_second}


EPS = 1e-06
THETA = 1000000.0
NS_A = 3.4445
NS_B = -4.775
NS_C = 2.0315
MOMENTUM = 0.95
BETA_ONE = 0.9
BETA_TWO = 0.95
GAIN_RATE = 0.2
ADAM_EPS = 1e-08
MASKED = -1e+30

@jax.custom_vjp
def reduced_precision(v):
    return lax.optimization_barrier(v.astype(jnp.bfloat16)).astype(jnp.float32)

@jax.custom_vjp
def reduced_precision_backward(v):
    return v

def low_keep(v):
    return (reduced_precision(v), None)

def low_pass(kept, grad):
    return (grad,)

def back_keep(v):
    return (v, None)

def back_low(kept, grad):
    return (reduced_precision(grad),)
reduced_precision.defvjp(low_keep, low_pass)
reduced_precision_backward.defvjp(back_keep, back_low)

def precise_product(left, right):
    return jnp.dot(left, right, precision=lax.Precision.HIGHEST)

def root_mean_square_norm(values, scaling):
    return values * lax.rsqrt(lax.optimization_barrier(jnp.mean(values * values, axis=-1, keepdims=True)) + EPS) * scaling

def rotary_embed(values, token_position):
    half_dim = values.shape[-1] // 2
    frequency = THETA ** (-jnp.arange(half_dim, dtype=jnp.float32) * 2.0 / values.shape[-1])
    angles = token_position.astype(jnp.float32)[:, None] * frequency[None, :]
    cosine = jnp.cos(angles)[:, None, :]
    sine_part = jnp.sin(angles)[:, None, :]
    lower_half = values[..., :half_dim]
    upper_half = values[..., half_dim:]
    return jnp.concatenate([lower_half * cosine - upper_half * sine_part, upper_half * cosine + lower_half * sine_part], axis=-1)

def sequence_layout(seq_lengths, every_row_packed):
    seq_lengths = seq_lengths.astype(jnp.int32)
    seq_ends = jnp.cumsum(seq_lengths).astype(jnp.int32)
    seq_starts = seq_ends - seq_lengths
    row_index = jnp.arange(every_row_packed, dtype=jnp.int32)
    segment = lax.optimization_barrier(jnp.sum((row_index[:, None] >= seq_ends[None, :]).astype(jnp.int32), axis=1)).astype(jnp.int32)
    chosen = segment[:, None] == jnp.arange(seq_lengths.shape[0], dtype=jnp.int32)[None, :]
    token_position = (row_index - lax.optimization_barrier(jnp.sum(jnp.where(chosen, seq_starts[None, :], 0), axis=1))).astype(jnp.int32)
    return (segment, token_position)

def group_layer(lowered, gains, block_in, seq_lengths):
    query_w, key_matrix, value_matrix, output_w, gate_w, up_w, down_w = lowered
    every_row_packed = block_in.shape[0]
    repeat_heads = QUERY_HEADS // KEY_VALUE_HEADS
    segment, token_position = sequence_layout(seq_lengths, every_row_packed)
    g_attn = gains[:MODEL_WIDTH]
    g_mlp = gains[MODEL_WIDTH:2 * MODEL_WIDTH]
    query_gradient = gains[2 * MODEL_WIDTH:2 * MODEL_WIDTH + HEAD_SIZE]
    g_key = gains[2 * MODEL_WIDTH + HEAD_SIZE:]
    first_normalized = reduced_precision(root_mean_square_norm(block_in, g_attn))
    query_rows = reduced_precision_backward(precise_product(first_normalized, query_w)).reshape(every_row_packed, QUERY_HEADS, HEAD_SIZE)
    key_unrotated = reduced_precision_backward(precise_product(first_normalized, key_matrix)).reshape(every_row_packed, KEY_VALUE_HEADS, HEAD_SIZE)
    value_projected = reduced_precision_backward(precise_product(first_normalized, value_matrix)).reshape(every_row_packed, KEY_VALUE_HEADS, HEAD_SIZE)
    query_rotated = reduced_precision(rotary_embed(root_mean_square_norm(query_rows, query_gradient), token_position)).reshape(every_row_packed, KEY_VALUE_HEADS, repeat_heads, HEAD_SIZE)
    k_rot = reduced_precision(rotary_embed(root_mean_square_norm(key_unrotated, g_key), token_position))
    v_low = reduced_precision(value_projected)
    scores = jnp.einsum('qkrd,skd->krqs', query_rotated, k_rot, precision=lax.Precision.HIGHEST) * HEAD_SIZE ** (-0.5)
    scores = reduced_precision_backward(scores)
    row_index = jnp.arange(every_row_packed, dtype=jnp.int32)
    allowed = (segment[:, None] == segment[None, :]) & (row_index[:, None] >= row_index[None, :])
    scores = jnp.where(allowed[None, None], scores, MASKED)
    row_max = lax.optimization_barrier(jnp.max(scores, axis=-1, keepdims=True))
    exponent = jnp.exp(scores - row_max)
    probability = reduced_precision(exponent / lax.optimization_barrier(jnp.sum(exponent, axis=-1, keepdims=True)))
    attended = jnp.einsum('krqs,skd->qkrd', probability, v_low, precision=lax.Precision.HIGHEST)
    attended = reduced_precision(reduced_precision_backward(attended.reshape(every_row_packed, QUERY_HEADS * HEAD_SIZE)))
    hidden_in = block_in + reduced_precision_backward(precise_product(attended, output_w))
    n_two = reduced_precision(root_mean_square_norm(hidden_in, g_mlp))
    gate_act = reduced_precision_backward(precise_product(n_two, gate_w))
    up_act = reduced_precision_backward(precise_product(n_two, up_w))
    inner_act = reduced_precision(jax.nn.silu(gate_act) * up_act)
    return hidden_in + reduced_precision_backward(precise_product(inner_act, down_w))

def forward(inputs, weights, gains, lengths):
    lowered = tuple((reduced_precision(matrix) for matrix in weights))
    groups = inputs.reshape(DP_GROUPS, GROUP_ROWS, MODEL_WIDTH)
    layer = jax.checkpoint(group_layer)

    def scan_step(carry, item):
        return (carry, layer(lowered, gains, item[0], item[1]))
    _, outputs = lax.scan(scan_step, jnp.zeros((), jnp.float32), (groups, lengths))
    return outputs.reshape(TOKEN_TOTAL, MODEL_WIDTH)

def orthogonal(matrix):
    current = matrix / (jnp.sqrt(jnp.sum(matrix * matrix)) + 1e-07)
    for turn in range(NS_ITERS):
        gram = precise_product(current.T, current)
        poly = NS_B * gram + NS_C * precise_product(gram, gram)
        current = NS_A * current + precise_product(current, poly)
    return current

def update_matrix(weight, gradient, moment, is_row, rate):
    renewed = MOMENTUM * moment + gradient
    if is_row:
        parts = renewed.reshape(N_TENSOR, renewed.shape[0] // N_TENSOR, renewed.shape[1]).transpose(0, 2, 1)
    else:
        parts = renewed.reshape(renewed.shape[0], N_TENSOR, renewed.shape[1] // N_TENSOR).transpose(1, 0, 2)
    ortho_parts = lax.map(orthogonal, parts)
    if is_row:
        placed = ortho_parts.transpose(0, 2, 1).reshape(weight.shape)
    else:
        placed = ortho_parts.transpose(1, 0, 2).reshape(weight.shape)
    return (renewed, weight - rate * placed)

def reference(tokens, out_grad, lengths, w_query, key_weight, value_weight, w_output, w_gate, w_up, w_down, momentum_query, key_momentum_buffer, value_momentum_buffer, momentum_output, momentum_gate, momentum_up, momentum_down, gains, gain_first, gain_second):
    inputs = tokens.astype(jnp.float32)
    weights = (w_query, key_weight, value_weight, w_output, w_gate, w_up, w_down)
    moments = (momentum_query, key_momentum_buffer, value_momentum_buffer, momentum_output, momentum_gate, momentum_up, momentum_down)
    rowwise = (False, False, False, True, False, False, True)
    rates = (1.0, 1.0, 1.0, math.sqrt(MODEL_WIDTH / (QUERY_HEADS * HEAD_SIZE // 16)), 1.0, 1.0, math.sqrt(MODEL_WIDTH / FF))

    def whole(inputs_in, weights_in, gains_in):
        return forward(inputs_in, weights_in, gains_in, lengths)
    result, pullback = jax.vjp(whole, inputs, weights, gains)
    tokens_grad, grads, gain_grad = pullback(out_grad.astype(jnp.float32))
    renewed_list = []
    updated_list = []
    for number in range(7):
        renewed, updated = update_matrix(weights[number], grads[number], moments[number], rowwise[number], rates[number])
        renewed_list.append(renewed)
        updated_list.append(updated)
    renewed_first = BETA_ONE * gain_first + (1.0 - BETA_ONE) * gain_grad
    renewed_second = BETA_TWO * gain_second + (1.0 - BETA_TWO) * gain_grad * gain_grad
    corrected_first = renewed_first / (1.0 - BETA_ONE ** ADAM_STEP)
    corrected_second = renewed_second / (1.0 - BETA_TWO ** ADAM_STEP)
    updated_gains = gains - GAIN_RATE * corrected_first / (jnp.sqrt(corrected_second) + ADAM_EPS)
    return (result.astype(jnp.bfloat16), tokens_grad, grads[0], grads[1], grads[2], grads[3], grads[4], grads[5], grads[6], renewed_list[0], renewed_list[1], renewed_list[2], renewed_list[3], renewed_list[4], renewed_list[5], renewed_list[6], updated_list[0], updated_list[1], updated_list[2], updated_list[3], updated_list[4], updated_list[5], updated_list[6], gain_grad, renewed_first, renewed_second, updated_gains)
```

```python
import math

import jax
import jax.numpy as jnp
from jax import lax
from jax.experimental import pallas as pl
from jax.experimental.pallas import tpu as pltpu
from jax.sharding import PartitionSpec as P

MODEL_WIDTH = 1024
QUERY_HEADS = 16
HEAD_SIZE = 128
FF = 3072
NS_ITERS = 5
ADAM_STEP = 10
TENSOR = 8
DATA = 16
ROWS = 128
SHARD = 64
BF = jnp.bfloat16
F32 = jnp.float32


EPS = 1e-06
THETA = 1000000.0
NS_A = 3.4445
NS_B = -4.775
NS_C = 2.0315
MOMENTUM = 0.95
BETA_ONE = 0.9
BETA_TWO = 0.95
GAIN_RATE = 0.2
ADAM_EPS = 1e-08
MASKED = -1e30


def root_mean_square_norm(values, scaling):
    return values * lax.rsqrt(jnp.mean(values * values, axis=-1, keepdims=True) + EPS) * scaling


def rotary_embed(values, token_position):
    half_dim = values.shape[-1] // 2
    frequency = THETA ** (-jnp.arange(half_dim, dtype=jnp.float32) * 2.0 / values.shape[-1])
    angles = token_position.astype(jnp.float32)[:, None] * frequency[None, :]
    cosine = jnp.cos(angles)[:, None, :]
    sine_part = jnp.sin(angles)[:, None, :]
    lower_half = values[..., :half_dim]
    upper_half = values[..., half_dim:]
    return jnp.concatenate(
        [
            lower_half * cosine - upper_half * sine_part,
            upper_half * cosine + lower_half * sine_part,
        ],
        axis=-1,
    )


def sequence_layout(seq_lengths, row_index):
    seq_ends = jnp.cumsum(seq_lengths)
    seq_starts = seq_ends - seq_lengths
    segment = jnp.sum((row_index[:, None] >= seq_ends[None, :]).astype(jnp.int32), axis=1)
    chosen = segment[:, None] == jnp.arange(seq_lengths.shape[0], dtype=jnp.int32)[None, :]
    token_position = row_index - jnp.sum(jnp.where(chosen, seq_starts[None, :], 0), axis=1)
    return (segment, token_position)


def whole_specs(number):
    return [pl.BlockSpec(memory_space=pltpu.VMEM)] * number


TURN_Z = ("tensor", [(t, t ^ 1) for t in range(TENSOR)])
UP_X = ("tensor", [(t, (t + 2) % TENSOR) for t in range(TENSOR)])
DOWN_X = ("tensor", [(t, (t - 2) % TENSOR) for t in range(TENSOR)])
TURN_CORE = ("dp", [(d, d ^ 1) for d in range(DATA)])
TURN_FAR = ("dp", [(d, d ^ 8) for d in range(DATA)])
TURN_BOTH = ("dp", [(d, d ^ 9) for d in range(DATA)])
UP_Y = ("dp", [(d, d // 8 * 8 + (d + 2) % 8) for d in range(DATA)])
DOWN_Y = ("dp", [(d, d // 8 * 8 + (d - 2) % 8) for d in range(DATA)])
OVER_TENSOR = (TURN_Z, UP_X, DOWN_X)
OVER_DATA = (TURN_FAR, UP_Y, DOWN_Y)
STEPS = (0, 0, -1, -1, 1, 1, 2, 2)


def send(block, link):
    return lax.ppermute(block, link[0], link[1])


def ring_spread(pair, up, down):
    half = pair.shape[0] // 2
    below = send(pair, up)
    above = send(pair, down)
    return [below, above, send(below[:half], up), send(above[half:], down)]


def ring_gather(block, links):
    turn, up, down = links
    pair = jnp.concatenate([block, send(block, turn)], axis=0)
    return [pair] + ring_spread(pair, up, down)


def ring_scatter(partial, rows, links):
    turn, up, down = links

    def slot(first, count=1):
        return partial[first * rows : (first + count) * rows]

    low = send(slot(6).astype(BF), down)
    high = send(slot(7).astype(BF), up)
    to_low = jnp.concatenate([slot(2) + low.astype(F32), slot(3).astype(F32)], axis=0).astype(BF)
    to_high = jnp.concatenate([slot(4).astype(F32), slot(5) + high.astype(F32)], axis=0).astype(BF)
    summed = slot(0, 2) + send(to_low, down).astype(F32) + send(to_high, up).astype(F32)
    return summed[:rows] + send(summed[rows:].astype(BF), turn).astype(F32)


def gather_tensor(block):
    return jnp.concatenate(ring_gather(block, OVER_TENSOR), axis=0)


def scatter_tensor(partial):
    return ring_scatter(partial, ROWS, OVER_TENSOR)


def slot_place(me, slot, core):
    far = jnp.bitwise_xor(me // 8, slot % 2)
    row = lax.rem(lax.rem(me // 2, 4) + STEPS[slot] + 4, 4)
    return pl.multiple_of((far * 8 + row * 2 + core) * SHARD, SHARD)


def place_kernel(me_ref, *refs):
    *near, other, out = refs
    me = me_ref[0]
    core = lax.rem(me, 2)
    slot = 0
    for part in near:
        for at in range(0, part.shape[0], SHARD):
            out[pl.ds(slot_place(me, slot, core), SHARD), :] = part[at : at + SHARD]
            out[pl.ds(slot_place(me, slot, 1 - core), SHARD), :] = other[
                slot * SHARD : (slot + 1) * SHARD
            ]
            slot += 1


def gather_data(block, me):
    near = ring_gather(block, OVER_DATA)
    other = send(jnp.concatenate(near, axis=0), TURN_CORE)
    return pl.pallas_call(
        place_kernel,
        in_specs=[pl.BlockSpec(memory_space=pltpu.SMEM)] + whole_specs(len(near) + 1),
        out_specs=whole_specs(1)[0],
        out_shape=jax.ShapeDtypeStruct((DATA * SHARD, block.shape[1]), BF),
        compiler_params=pltpu.CompilerParams(vmem_limit_bytes=32 * 2**20),
        name="place_weights",
    )(me, *near, other)


def split_kernel(me_ref, whole_ref, keep_ref, send_ref):
    me = me_ref[0]
    core = lax.rem(me, 2)
    for slot in range(8):
        at = slice(slot * SHARD, (slot + 1) * SHARD)
        keep_ref[at] = whole_ref[pl.ds(slot_place(me, slot, core), SHARD), :]
        send_ref[at] = whole_ref[pl.ds(slot_place(me, slot, 1 - core), SHARD), :].astype(BF)


SCALAR = pl.BlockSpec(memory_space=pltpu.SMEM)
BLOCK = 256
ALL_ROWS = TENSOR * ROWS
SCORE_SCALE = HEAD_SIZE**-0.5


def cost(flops, moved):
    return pl.CostEstimate(flops=int(flops), bytes_accessed=int(moved), transcendentals=0)


def room(megabytes):
    return pltpu.CompilerParams(vmem_limit_bytes=megabytes * 2**20)


def inverse_size(values):
    return lax.rsqrt(jnp.mean(values * values, axis=-1, keepdims=True) + EPS)


def scores_of(keys, queries, key_row, query_row, query_start):
    product = dot_f32(keys, queries, ((1,), (1,))) * SCORE_SCALE
    allowed = (key_row >= query_start) & (key_row <= query_row)
    return jnp.where(allowed, product, MASKED)


def forward_kernel(
    rows_ref, weight_ref, out_weight_ref, cos_ref, sin_ref, gain_ref, key_row_ref, row_ref, start_ref,
    raw_ref, low_ref, attended_ref, log_ref, part_ref, value_t,
):
    def project(block, carry):
        at = pl.ds(pl.multiple_of(block * BLOCK, BLOCK), BLOCK)
        product = dot_f32(rows_ref[at, :], weight_ref[...], ((1,), (0,)))
        raw_ref[at, :] = product
        cosine, sine = cos_ref[at, :], sin_ref[at, :]
        for head in range(3):
            lanes = slice(head * HEAD_SIZE, (head + 1) * HEAD_SIZE)
            values = product[:, lanes]
            gain = gain_ref[head // 2 : head // 2 + 1, :]
            scaled = values * inverse_size(values) * gain
            turned = scaled * cosine + pltpu.roll(scaled, HEAD_SIZE // 2, 1) * sine
            low_ref[at, lanes] = turned.astype(BF)
        low_ref[at, 3 * HEAD_SIZE :] = product[:, 3 * HEAD_SIZE :].astype(BF)
        return carry

    lax.fori_loop(0, ALL_ROWS // BLOCK, project, 0)
    value_t[...] = low_ref[:, 3 * HEAD_SIZE :].T
    for block in range(ALL_ROWS // BLOCK):
        at = slice(block * BLOCK, (block + 1) * BLOCK)
        for head in range(2):
            lanes = slice(head * HEAD_SIZE, (head + 1) * HEAD_SIZE)
            scores = scores_of(
                low_ref[:, 2 * HEAD_SIZE : 3 * HEAD_SIZE], low_ref[at, lanes],
                key_row_ref[...], row_ref[:, at], start_ref[:, at],
            )
            top = jnp.max(scores, axis=0, keepdims=True)
            exponent = jnp.exp(scores - top)
            summed = jnp.sum(exponent, axis=0, keepdims=True)
            probability = (exponent * (1.0 / summed)).astype(BF)
            out_t = dot_f32(value_t[...], probability, ((1,), (0,)))
            attended_ref[at, lanes] = out_t.T.astype(BF)
            log_ref[head : head + 1, at] = top + jnp.log(summed)
        part_ref[at, :] = dot_f32(
            attended_ref[at, :], out_weight_ref[...], ((1,), (1,))
        ).astype(BF)


def mlp_kernel(
    slot_ref, rows_ref, grad_ref, weight_ref, hid_ref, d_ref, back_ref, part_ref
):
    def turn(block, carry):
        at = pl.ds(pl.multiple_of(block * BLOCK, BLOCK), BLOCK)
        grads = jnp.concatenate([grad_ref[slot_ref[2 * block]], grad_ref[slot_ref[2 * block + 1]]])
        both = dot_f32(rows_ref[at, :], weight_ref[:, :768], ((1,), (0,)))
        gate, up = both[:, :384], both[:, 384:]
        sigmoid = jax.nn.sigmoid(gate)
        silu = gate * sigmoid
        hid = (silu * up).astype(BF)
        hid_ref[at, :] = hid
        d_hid = dot_f32(grads, weight_ref[:, 768:], ((1,), (0,)))
        d_gate = (d_hid * up * sigmoid * (1.0 + gate * (1.0 - sigmoid))).astype(BF)
        d_both = jnp.concatenate([d_gate, (d_hid * silu).astype(BF)], axis=1)
        d_ref[at, :] = d_both
        back_ref[at, :] = dot_f32(d_both, weight_ref[:, :768], ((1,), (1,))).astype(BF)
        part_ref[at, :] = dot_f32(hid, weight_ref[:, 768:], ((1,), (1,))).astype(BF)
        return carry

    lax.fori_loop(0, ALL_ROWS // BLOCK, turn, 0)


def split_rows(me, whole, keep_ref, send_ref):
    core = lax.rem(me, 2)
    for slot in range(8):
        at = slice(slot * SHARD, (slot + 1) * SHARD)
        keep_ref[at] = whole[pl.ds(slot_place(me, slot, core), SHARD), :]
        send_ref[at] = whole[pl.ds(slot_place(me, slot, 1 - core), SHARD), :].astype(BF)


def mlp_grads_kernel(
    me_ref, slot_ref, rows_ref, grad_ref, hid_ref, d_ref, keep_ref, send_ref, whole, grads
):
    for slot in range(TENSOR):
        grads[slot * ROWS : (slot + 1) * ROWS] = grad_ref[slot_ref[slot]]
    for block in range(MODEL_WIDTH // BLOCK):
        at = slice(block * BLOCK, (block + 1) * BLOCK)
        whole[at, :768] = dot_f32(rows_ref[:, at], d_ref[...], ((0,), (0,)))
        whole[at, 768:] = dot_f32(grads[:, at], hid_ref[...], ((0,), (0,)))
    split_rows(me_ref[0], whole, keep_ref, send_ref)


def attn_grads_kernel(me_ref, rows_ref, d_ref, back_ref, attended_ref, keep_ref, send_ref, whole):
    for block in range(MODEL_WIDTH // BLOCK):
        at = slice(block * BLOCK, (block + 1) * BLOCK)
        whole[at, :512] = dot_f32(rows_ref[:, at], d_ref[...], ((0,), (0,)))
        whole[at, 512:] = dot_f32(back_ref[:, at], attended_ref[...], ((0,), (0,)))
    split_rows(me_ref[0], whole, keep_ref, send_ref)


def backward_kernel(
    back_ref, raw_ref, low_ref, log_ref, weight_ref, out_weight_ref, cos_ref, sin_ref, gain_ref,
    key_row_ref, row_ref, start_ref,
    d_ref, gain_grad_ref, part_ref, d_key, d_value, key_t,
):
    keys = slice(2 * HEAD_SIZE, 3 * HEAD_SIZE)
    values = slice(3 * HEAD_SIZE, 4 * HEAD_SIZE)
    key_t[...] = low_ref[:, keys].T
    d_key[...] = jnp.zeros_like(d_key)
    d_value[...] = jnp.zeros_like(d_value)

    def through_norm(turned, raw, cosine, sine, gain):
        scaled = turned * cosine + pltpu.roll(turned * sine, HEAD_SIZE // 2, 1)
        inverse = inverse_size(raw)
        weighted = scaled * gain
        mean = jnp.mean(weighted * raw, axis=-1, keepdims=True)
        grad = inverse * weighted - raw * (inverse * inverse * inverse * mean)
        return grad.astype(BF), jnp.sum(scaled * raw * inverse, axis=0, keepdims=True)

    query_gain_grad = jnp.zeros((1, HEAD_SIZE), F32)
    for block in range(ALL_ROWS // BLOCK):
        at = slice(block * BLOCK, (block + 1) * BLOCK)
        d_attended = dot_f32(back_ref[at, :], out_weight_ref[...], ((1,), (0,))).astype(BF)
        for head in range(2):
            lanes = slice(head * HEAD_SIZE, (head + 1) * HEAD_SIZE)
            queries = low_ref[at, lanes]
            d_out = d_attended[:, lanes]
            scores = scores_of(
                low_ref[:, keys], queries, key_row_ref[...], row_ref[:, at], start_ref[:, at]
            )
            probability = jnp.exp(scores - log_ref[head : head + 1, at])
            d_prob = dot_f32(low_ref[:, values], d_out, ((1,), (1,)))
            row_dot = jnp.sum(probability * d_prob, axis=0, keepdims=True)
            d_score = (probability * (d_prob - row_dot)).astype(BF)
            d_value[...] += dot_f32(probability.astype(BF), d_out, ((1,), (0,)))
            d_key[...] += dot_f32(d_score, queries, ((1,), (0,)))
            d_query_t = dot_f32(key_t[...], d_score, ((1,), (0,)))
            grad, gain_part = through_norm(
                d_query_t.T * SCORE_SCALE, raw_ref[at, lanes], cos_ref[at, :], sin_ref[at, :],
                gain_ref[0:1, :],
            )
            d_ref[at, lanes] = grad
            query_gain_grad = query_gain_grad + gain_part
    key_gain_grad = jnp.zeros((1, HEAD_SIZE), F32)
    for block in range(ALL_ROWS // BLOCK):
        at = slice(block * BLOCK, (block + 1) * BLOCK)
        grad, gain_part = through_norm(
            d_key[at, :] * SCORE_SCALE, raw_ref[at, keys], cos_ref[at, :], sin_ref[at, :],
            gain_ref[1:2, :],
        )
        d_ref[at, keys] = grad
        d_ref[at, values] = d_value[at, :].astype(BF)
        key_gain_grad = key_gain_grad + gain_part
        part_ref[at, :] = dot_f32(d_ref[at, :], weight_ref[...], ((1,), (1,))).astype(BF)
    gain_grad_ref[0:1, :] = query_gain_grad
    gain_grad_ref[1:2, :] = key_gain_grad


def scatter_data(pair):
    keep, other = pair
    return ring_scatter(keep + send(other, TURN_CORE).astype(F32), SHARD, OVER_DATA)


def shape(rows, columns, kind):
    return jax.ShapeDtypeStruct((rows, columns), kind)


def split_shapes(width):
    return [shape(8 * SHARD, width, F32), shape(8 * SHARD, width, BF)]


def pack_kernel(me_ref, rows_ref, *outs):
    me = me_ref[0]
    kind = lax.rem(me, 2) + 2 * (me // 8)
    width = outs[0].shape[1]
    for turn in range(4):
        number = jnp.minimum(jnp.bitwise_xor(kind, turn), 2)
        for choice in range(3):

            @pl.when(number == choice)
            def _(turn=turn, choice=choice):
                outs[turn][...] = rows_ref[:, choice * width : (choice + 1) * width].astype(BF)


def split_low(value):
    high = value.astype(BF)
    return high, (value - high.astype(F32)).astype(BF)


def dot_f32(left, right, dims):
    return lax.dot_general(left, right, (dims, ((), ())), preferred_element_type=F32)


def orthogonal_kernel(paired, me_ref, *refs):
    parts, outs, current = refs[:5], refs[5:9], refs[9]
    me = me_ref[0]
    kind = lax.rem(me, 2) + 2 * (me // 8)
    width = outs[0].shape[1]
    at = 0
    for part in parts:
        current[at : at + part.shape[0]] = part[...].astype(F32)
        at += part.shape[0]
    matrix = current[...]
    columns = jnp.sum(matrix * matrix, axis=0, keepdims=True)
    size = jnp.sum(columns, keepdims=True)
    if paired is not None:
        place = lax.broadcasted_iota(jnp.int32, (1, width), 1) < width // 2
        first = jnp.sum(jnp.where(place, columns, 0.0), keepdims=True)
        second = jnp.sum(jnp.where(place, 0.0, columns), keepdims=True)
        size = jnp.where(kind == paired, jnp.where(place, first, second), size)
        down = lax.broadcasted_iota(jnp.int32, (width, width), 0) < width // 2
        across = lax.broadcasted_iota(jnp.int32, (width, width), 1) < width // 2
        apart = (down != across) & (kind == paired)
    current[...] = matrix / (jnp.sqrt(size) + 1e-07)

    def polynomial(high, low):
        cross = dot_f32(high, low, ((0,), (0,)))
        gram = dot_f32(high, high, ((0,), (0,))) + (cross + cross.T)
        if paired is not None:
            gram = jnp.where(apart, 0.0, gram)
        gram_high, gram_low = split_low(gram)
        cross = dot_f32(gram_high, gram_low, ((1,), (0,)))
        square = dot_f32(gram_high, gram_high, ((1,), (0,))) + (cross + cross.T)
        return split_low(NS_B * gram + NS_C * square)

    def moved(value, high, low, poly_high, poly_low):
        change = dot_f32(high, poly_high, ((1,), (0,)))
        change = change + dot_f32(high, poly_low, ((1,), (0,)))
        change = change + dot_f32(low, poly_high, ((1,), (0,)))
        return NS_A * value + change

    def turn(_, carry):
        value = current[...]
        high, low = split_low(value)
        poly_high, poly_low = polynomial(high, low)
        current[...] = moved(value, high, low, poly_high, poly_low)
        return carry

    lax.fori_loop(0, NS_ITERS - 1, turn, 0)
    high, low = split_low(current[...])
    poly_high, poly_low = polynomial(high, low)
    rows = 4 * SHARD
    last = moved(current[:rows], high[:rows], low[:rows], poly_high, poly_low)
    for number in range(4):
        outs[number][...] = last[number * SHARD : (number + 1) * SHARD].astype(BF)


def update_kernel(rates, me_ref, master_ref, *refs):
    turned, out = refs[:4], refs[4]
    me = me_ref[0]
    kind = lax.rem(me, 2) + 2 * (me // 8)
    width = turned[0].shape[1]
    for turn in range(4):
        for number in range(3):

            @pl.when(jnp.bitwise_xor(kind, turn) == number)
            def _(turn=turn, number=number):
                at = slice(number * width, (number + 1) * width)
                out[:, at] = master_ref[:, at] - rates[number] * turned[turn][...].astype(F32)


def muon(me, renewed, masters, rates, paired):
    width = renewed.shape[1] // 3
    scalar = [pl.BlockSpec(memory_space=pltpu.SMEM)]
    limit = pltpu.CompilerParams(vmem_limit_bytes=48 * 2**20)
    turns = (TURN_CORE, TURN_FAR, TURN_BOTH)
    quarter = jax.ShapeDtypeStruct((SHARD, width), BF)
    packed = pl.pallas_call(
        pack_kernel,
        in_specs=scalar + whole_specs(1),
        out_specs=whole_specs(4),
        out_shape=[quarter] * 4,
        compiler_params=limit,
        name="muon_pack",
    )(me, renewed)
    own = jnp.concatenate(
        [packed[0]] + [send(block, turn) for block, turn in zip(packed[1:], turns)], axis=0
    )
    parts = [own] + ring_spread(own, UP_Y, DOWN_Y)
    turned = pl.pallas_call(
        lambda *refs: orthogonal_kernel(paired, *refs),
        in_specs=scalar + whole_specs(5),
        out_specs=whole_specs(4),
        out_shape=[quarter] * 4,
        scratch_shapes=[pltpu.VMEM((DATA * SHARD, width), F32)],
        compiler_params=limit,
        name="muon_turns",
    )(me, *parts)
    back = [turned[0]] + [send(block, turn) for block, turn in zip(turned[1:], turns)]
    return pl.pallas_call(
        lambda *refs: update_kernel(rates, *refs),
        in_specs=scalar + whole_specs(5),
        out_specs=whole_specs(1)[0],
        out_shape=jax.ShapeDtypeStruct(masters.shape, F32),
        compiler_params=limit,
        name="muon_update",
    )(me, masters, *back)


def local(
    tokens,
    out_grad,
    lengths,
    w_query,
    key_weight,
    value_weight,
    w_output,
    w_gate,
    w_up,
    w_down,
    momentum_query,
    key_momentum_buffer,
    value_momentum_buffer,
    momentum_output,
    momentum_gate,
    momentum_up,
    momentum_down,
    gains,
    gain_first,
    gain_second,
):
    tensor_index = lax.axis_index("tensor")
    data_index = lax.axis_index("dp")
    me = data_index.astype(jnp.int32).reshape(1)
    attn_masters = jnp.concatenate([w_query, key_weight, value_weight, w_output.T], axis=1)
    mlp_masters = jnp.concatenate([w_gate, w_up, w_down.T], axis=1)
    attn_moments = jnp.concatenate(
        [momentum_query, key_momentum_buffer, value_momentum_buffer, momentum_output.T], axis=1
    )
    mlp_moments = jnp.concatenate([momentum_gate, momentum_up, momentum_down.T], axis=1)
    g_attn = gains[:MODEL_WIDTH]
    g_mlp = gains[MODEL_WIDTH : 2 * MODEL_WIDTH]
    query_gain = gains[2 * MODEL_WIDTH : 2 * MODEL_WIDTH + HEAD_SIZE]
    g_key = gains[2 * MODEL_WIDTH + HEAD_SIZE :]
    inputs = tokens.astype(F32)
    first_normalized = gather_tensor(root_mean_square_norm(inputs, g_attn).astype(BF))
    attn_weights = gather_data(attn_masters.astype(BF), me)
    mlp_lowered, first_normalized = lax.optimization_barrier(
        (mlp_masters.astype(BF), first_normalized)
    )
    mlp_weights = gather_data(mlp_lowered, me)
    slots = [
        lax.rem(tensor_index // 2 + STEPS[s] + 4, 4) * 2 + jnp.bitwise_xor(tensor_index % 2, s % 2)
        for s in range(TENSOR)
    ]
    in_order = lax.all_gather(out_grad, "tensor", axis=0)
    qkv_full, output_full = attn_weights[:, :512], attn_weights[:, 512:]
    slot_list = jnp.stack(slots).astype(jnp.int32)
    row_index = jnp.concatenate([slot * ROWS + jnp.arange(ROWS, dtype=jnp.int32) for slot in slots])
    segment, token_position = sequence_layout(lengths[0], row_index)
    half = HEAD_SIZE // 2
    frequency = THETA ** (-jnp.arange(half, dtype=F32) * 2.0 / HEAD_SIZE)
    angles = token_position.astype(F32)[:, None] * frequency[None, :]
    cosine, sine = jnp.cos(angles), jnp.sin(angles)
    cosine = jnp.concatenate([cosine, cosine], axis=1)
    sine = jnp.concatenate([-sine, sine], axis=1)
    head_gains = jnp.stack([query_gain, g_key])
    key_row = row_index[:, None]
    query_row = row_index[None, :]
    query_start = (row_index - token_position)[None, :]
    raw, rotated, attn_low, logsum, branch_part = pl.pallas_call(
        forward_kernel,
        in_specs=whole_specs(9),
        out_specs=whole_specs(5),
        out_shape=[
            shape(ALL_ROWS, 512, F32),
            shape(ALL_ROWS, 512, BF),
            shape(ALL_ROWS, 256, BF),
            shape(2, ALL_ROWS, F32),
            shape(ALL_ROWS, MODEL_WIDTH, BF),
        ],
        scratch_shapes=[pltpu.VMEM((HEAD_SIZE, ALL_ROWS), BF)],
        compiler_params=room(48),
        cost_estimate=cost(2.7e9, 12e6),
        name="attention_forward",
    )(
        first_normalized, qkv_full, output_full, cosine, sine, head_gains,
        key_row, query_row, query_start,
    )
    branch_out = scatter_tensor(branch_part)
    hidden_in = inputs + branch_out
    n_two = gather_tensor(root_mean_square_norm(hidden_in, g_mlp).astype(BF))
    inner_act, d_both, back_part, mlp_part = pl.pallas_call(
        mlp_kernel,
        in_specs=[SCALAR] + whole_specs(3),
        out_specs=whole_specs(4),
        out_shape=[
            shape(ALL_ROWS, 384, BF),
            shape(ALL_ROWS, 768, BF),
            shape(ALL_ROWS, MODEL_WIDTH, BF),
            shape(ALL_ROWS, MODEL_WIDTH, BF),
        ],
        compiler_params=room(48),
        cost_estimate=cost(4.9e9, 12e6),
        name="mlp_both_ways",
    )(slot_list, n_two, in_order, mlp_weights)
    d_norm_two = scatter_tensor(back_part)
    mlp_grads = pl.pallas_call(
        mlp_grads_kernel,
        in_specs=[SCALAR] * 2 + whole_specs(4),
        out_specs=whole_specs(2),
        out_shape=split_shapes(1152),
        scratch_shapes=[
            pltpu.VMEM((MODEL_WIDTH, 1152), F32),
            pltpu.VMEM((ALL_ROWS, MODEL_WIDTH), BF),
        ],
        compiler_params=room(48),
        cost_estimate=cost(2.4e9, 10e6),
        name="mlp_grads",
    )(me, slot_list, n_two, in_order, inner_act, d_both)
    mlp_reduced = scatter_data(mlp_grads)
    mlp_renewed = MOMENTUM * mlp_moments + mlp_reduced
    mlp_updated = muon(
        me, mlp_renewed, mlp_masters, (1.0, 1.0, math.sqrt(MODEL_WIDTH / FF)), None
    )
    _, norm_two_back = jax.vjp(root_mean_square_norm, hidden_in, g_mlp)
    d_hidden_in, dg_mlp = norm_two_back(d_norm_two)
    d_residual = out_grad.astype(F32) + d_hidden_in
    residual_rows = gather_tensor(d_residual.astype(BF))
    d_qkv, head_gain_grads, d_norm_part = pl.pallas_call(
        backward_kernel,
        in_specs=whole_specs(12),
        out_specs=whole_specs(3),
        out_shape=[
            shape(ALL_ROWS, 512, BF),
            shape(2, HEAD_SIZE, F32),
            shape(ALL_ROWS, MODEL_WIDTH, BF),
        ],
        scratch_shapes=[
            pltpu.VMEM((ALL_ROWS, HEAD_SIZE), F32),
            pltpu.VMEM((ALL_ROWS, HEAD_SIZE), F32),
            pltpu.VMEM((HEAD_SIZE, ALL_ROWS), BF),
        ],
        compiler_params=room(48),
        cost_estimate=cost(4.2e9, 14e6),
        name="attention_backward",
    )(
        residual_rows, raw, rotated, logsum, qkv_full, output_full, cosine, sine, head_gains,
        key_row, query_row, query_start,
    )
    attn_grads = pl.pallas_call(
        attn_grads_kernel,
        in_specs=[SCALAR] + whole_specs(4),
        out_specs=whole_specs(2),
        out_shape=split_shapes(768),
        scratch_shapes=[pltpu.VMEM((MODEL_WIDTH, 768), F32)],
        compiler_params=room(48),
        cost_estimate=cost(1.6e9, 10e6),
        name="attention_grads",
    )(me, first_normalized, d_qkv, residual_rows, attn_low)
    attn_reduced = scatter_data(attn_grads)
    attn_renewed = MOMENTUM * attn_moments + attn_reduced
    attn_updated = muon(
        me,
        attn_renewed,
        attn_masters,
        (1.0, 1.0, math.sqrt(MODEL_WIDTH / (QUERY_HEADS * HEAD_SIZE // 16))),
        1,
    )
    both = scatter_tensor(jnp.concatenate([d_norm_part, mlp_part], axis=1))
    d_norm_one, mlp_out = both[:, :MODEL_WIDTH], both[:, MODEL_WIDTH:]
    result = (hidden_in + mlp_out).astype(BF)
    _, norm_one_back = jax.vjp(root_mean_square_norm, inputs, g_attn)
    d_inputs, dg_attn = norm_one_back(d_norm_one)
    tokens_grad = d_residual + d_inputs
    gain_grad = jnp.concatenate([dg_attn, dg_mlp, head_gain_grads[0], head_gain_grads[1]])
    for axis, count in (("tensor", TENSOR), ("dp", DATA)):
        turn = 1
        while turn < count:
            gain_grad = gain_grad + send(gain_grad, (axis, [(i, i ^ turn) for i in range(count)]))
            turn *= 2
    renewed_first = BETA_ONE * gain_first + (1.0 - BETA_ONE) * gain_grad
    renewed_second = BETA_TWO * gain_second + (1.0 - BETA_TWO) * gain_grad * gain_grad
    corrected_first = renewed_first / (1.0 - BETA_ONE**ADAM_STEP)
    corrected_second = renewed_second / (1.0 - BETA_TWO**ADAM_STEP)
    updated_gains = gains - GAIN_RATE * corrected_first / (jnp.sqrt(corrected_second) + ADAM_EPS)

    def unpack(attn, mlp):
        return (
            attn[:, :256],
            attn[:, 256:384],
            attn[:, 384:512],
            attn[:, 512:].T,
            mlp[:, :384],
            mlp[:, 384:768],
            mlp[:, 768:].T,
        )

    return (
        result,
        tokens_grad,
        *unpack(attn_reduced, mlp_reduced),
        *unpack(attn_renewed, mlp_renewed),
        *unpack(attn_updated, mlp_updated),
        gain_grad,
        renewed_first,
        renewed_second,
        updated_gains,
    )


def solution(mesh):
    placed = (
        P(("dp", "tensor"), None),
        P(("dp", "tensor"), None),
        P("dp", None),
        P("dp", "tensor"),
        P("dp", "tensor"),
        P("dp", "tensor"),
        P("tensor", "dp"),
        P("dp", "tensor"),
        P("dp", "tensor"),
        P("tensor", "dp"),
        P("dp", "tensor"),
        P("dp", "tensor"),
        P("dp", "tensor"),
        P("tensor", "dp"),
        P("dp", "tensor"),
        P("dp", "tensor"),
        P("tensor", "dp"),
        P(),
        P(),
        P(),
    )
    return jax.shard_map(
        local,
        mesh=mesh,
        in_specs=placed,
        out_specs=(
            P(("dp", "tensor"), None),
            P(("dp", "tensor"), None),
            P("dp", "tensor"),
            P("dp", "tensor"),
            P("dp", "tensor"),
            P("tensor", "dp"),
            P("dp", "tensor"),
            P("dp", "tensor"),
            P("tensor", "dp"),
            P("dp", "tensor"),
            P("dp", "tensor"),
            P("dp", "tensor"),
            P("tensor", "dp"),
            P("dp", "tensor"),
            P("dp", "tensor"),
            P("tensor", "dp"),
            P("dp", "tensor"),
            P("dp", "tensor"),
            P("dp", "tensor"),
            P("tensor", "dp"),
            P("dp", "tensor"),
            P("dp", "tensor"),
            P("tensor", "dp"),
            P(),
            P(),
            P(),
            P(),
        ),
        check_vma=False,
    )
```

```python
import functools
import math

import jax
import jax.numpy as jnp
from jax import lax
from jax.experimental import pallas as pl
from jax.experimental.pallas import tpu as pltpu
from jax.sharding import PartitionSpec as P

MODEL_WIDTH = 1024
QUERY_HEADS = 16
HEAD_SIZE = 128
FF = 3072
NS_ITERS = 5
ADAM_STEP = 10
TENSOR = 8
DATA = 16
ROWS = 128
SHARD = 64
BF = jnp.bfloat16
F32 = jnp.float32


EPS = 1e-06
THETA = 1000000.0
NS_A = 3.4445
NS_B = -4.775
NS_C = 2.0315
MOMENTUM = 0.95
BETA_ONE = 0.9
BETA_TWO = 0.95
GAIN_RATE = 0.2
ADAM_EPS = 1e-08
MASKED = -1e30


def root_mean_square_norm(values, scaling):
    return values * lax.rsqrt(jnp.mean(values * values, axis=-1, keepdims=True) + EPS) * scaling


def rotary_embed(values, token_position):
    half_dim = values.shape[-1] // 2
    frequency = THETA ** (-jnp.arange(half_dim, dtype=jnp.float32) * 2.0 / values.shape[-1])
    angles = token_position.astype(jnp.float32)[:, None] * frequency[None, :]
    cosine = jnp.cos(angles)[:, None, :]
    sine_part = jnp.sin(angles)[:, None, :]
    lower_half = values[..., :half_dim]
    upper_half = values[..., half_dim:]
    return jnp.concatenate(
        [
            lower_half * cosine - upper_half * sine_part,
            upper_half * cosine + lower_half * sine_part,
        ],
        axis=-1,
    )


def sequence_layout(seq_lengths, row_index):
    seq_ends = jnp.cumsum(seq_lengths)
    seq_starts = seq_ends - seq_lengths
    segment = jnp.sum((row_index[:, None] >= seq_ends[None, :]).astype(jnp.int32), axis=1)
    chosen = segment[:, None] == jnp.arange(seq_lengths.shape[0], dtype=jnp.int32)[None, :]
    token_position = row_index - jnp.sum(jnp.where(chosen, seq_starts[None, :], 0), axis=1)
    return (segment, token_position)


def whole_specs(number):
    return [pl.BlockSpec(memory_space=pltpu.VMEM)] * number


TURN_Z = ("tensor", [(t, t ^ 1) for t in range(TENSOR)])
UP_X = ("tensor", [(t, (t + 2) % TENSOR) for t in range(TENSOR)])
DOWN_X = ("tensor", [(t, (t - 2) % TENSOR) for t in range(TENSOR)])
TURN_CORE = ("dp", [(d, d ^ 1) for d in range(DATA)])
TURN_FAR = ("dp", [(d, d ^ 8) for d in range(DATA)])
TURN_BOTH = ("dp", [(d, d ^ 9) for d in range(DATA)])
UP_Y = ("dp", [(d, d // 8 * 8 + (d + 2) % 8) for d in range(DATA)])
DOWN_Y = ("dp", [(d, d // 8 * 8 + (d - 2) % 8) for d in range(DATA)])
OVER_TENSOR = (TURN_Z, UP_X, DOWN_X)
OVER_DATA = (TURN_FAR, UP_Y, DOWN_Y)
STEPS = (0, 0, -1, -1, 1, 1, 2, 2)


def send(block, link):
    return lax.ppermute(block, link[0], link[1])


def plain(*payload):
    return payload


def ring_spread(pair, up, down, beside=plain):
    half = pair.shape[0] // 2
    below = send(pair, up)
    above = send(pair, down)
    first, second = beside(below[:half], above[half:])
    return [below, above, send(first, up), send(second, down)]


def ring_gather(block, links):
    turn, up, down = links
    pair = jnp.concatenate([block, send(block, turn)], axis=0)
    return [pair] + ring_spread(pair, up, down)


def ring_scatter(parts, links, beside=plain):
    turn, up, down = links
    own, below, above, low, high = parts
    rows = low.shape[0]
    low, high = beside(low.astype(BF), high.astype(BF))
    low = send(low, down).astype(F32)
    high = send(high, up).astype(F32)
    to_low = jnp.concatenate([below[:rows] + low, below[rows:].astype(F32)], axis=0).astype(BF)
    to_high = jnp.concatenate([above[:rows].astype(F32), above[rows:] + high], axis=0).astype(BF)
    to_low, to_high = beside(to_low, to_high)
    summed = own + send(to_low, down).astype(F32) + send(to_high, up).astype(F32)
    (last,) = beside(summed[rows:].astype(BF))
    return summed[:rows] + send(last, turn).astype(F32)


def part_rows(rows):
    return (2 * rows, 2 * rows, 2 * rows, rows, rows)


def block_of(parts, block):
    if block < 3:
        return parts[block][...]
    return jnp.concatenate([parts[3][...], parts[4][...]], axis=0)


def store_block(parts, block, lanes, value):
    if block < 3:
        parts[block][:, lanes] = value
    else:
        parts[3][:, lanes] = value[:ROWS]
        parts[4][:, lanes] = value[ROWS:]


def slot_place(me, slot, core):
    far = jnp.bitwise_xor(me // 8, slot % 2)
    row = lax.rem(lax.rem(me // 2, 4) + STEPS[slot] + 4, 4)
    return pl.multiple_of((far * 8 + row * 2 + core) * SHARD, SHARD)


def place_kernel(me_ref, *refs):
    near, other, outs = refs[:5], refs[5], refs[6:]
    me = me_ref[0]
    core = lax.rem(me, 2)
    slot = 0
    for part in near:
        for at in range(0, part.shape[0], SHARD):
            here = pl.ds(slot_place(me, slot, core), SHARD)
            there = pl.ds(slot_place(me, slot, 1 - core), SHARD)
            first = 0
            for out in outs:
                lanes = slice(first, first + out.shape[1])
                out[here, :] = part[at : at + SHARD, lanes]
                out[there, :] = other[slot * SHARD : (slot + 1) * SHARD, lanes]
                first += out.shape[1]
            slot += 1


def gather_data(block, me, widths):
    near = ring_gather(block, OVER_DATA)
    other = send(jnp.concatenate(near, axis=0), TURN_CORE)
    return pl.pallas_call(
        place_kernel,
        in_specs=[pl.BlockSpec(memory_space=pltpu.SMEM)] + whole_specs(6),
        out_specs=whole_specs(len(widths)),
        out_shape=[jax.ShapeDtypeStruct((DATA * SHARD, width), BF) for width in widths],
        compiler_params=pltpu.CompilerParams(vmem_limit_bytes=32 * 2**20),
        name="place_weights",
    )(me, *near, other)


SCALAR = pl.BlockSpec(memory_space=pltpu.SMEM)
BLOCK = 256
ALL_ROWS = TENSOR * ROWS
SCORE_SCALE = HEAD_SIZE**-0.5


def cost(flops, moved):
    return pl.CostEstimate(flops=int(flops), bytes_accessed=int(moved), transcendentals=0)


def room(megabytes):
    return pltpu.CompilerParams(vmem_limit_bytes=megabytes * 2**20)


def inverse_size(values):
    return lax.rsqrt(jnp.mean(values * values, axis=-1, keepdims=True) + EPS)


def scores_of(keys, queries, key_row, query_row, query_start):
    product = dot_f32(keys, queries, ((1,), (1,))) * SCORE_SCALE
    allowed = (key_row >= query_start) & (key_row <= query_row)
    return jnp.where(allowed, product, MASKED)


def forward_kernel(*refs):
    rows, refs = refs[:5], refs[5:]
    weight_ref, out_weight_ref, cos_ref, sin_ref, gain_ref, key_row_ref, row_ref, start_ref = refs[:8]
    raw_ref, low_ref, attended_ref, log_ref = refs[8:12]
    parts, value_t = refs[12:17], refs[17]
    for block in range(ALL_ROWS // BLOCK):
        at = slice(block * BLOCK, (block + 1) * BLOCK)
        product = dot_f32(block_of(rows, block), weight_ref[...], ((1,), (0,)))
        raw_ref[at, :] = product
        cosine, sine = cos_ref[at, :], sin_ref[at, :]
        for head in range(3):
            lanes = slice(head * HEAD_SIZE, (head + 1) * HEAD_SIZE)
            values = product[:, lanes]
            gain = gain_ref[head // 2 : head // 2 + 1, :]
            scaled = values * inverse_size(values) * gain
            turned = scaled * cosine + pltpu.roll(scaled, HEAD_SIZE // 2, 1) * sine
            low_ref[at, lanes] = turned.astype(BF)
        low_ref[at, 3 * HEAD_SIZE :] = product[:, 3 * HEAD_SIZE :].astype(BF)
    value_t[...] = low_ref[:, 3 * HEAD_SIZE :].T
    for block in range(ALL_ROWS // BLOCK):
        at = slice(block * BLOCK, (block + 1) * BLOCK)
        for head in range(2):
            lanes = slice(head * HEAD_SIZE, (head + 1) * HEAD_SIZE)
            scores = scores_of(
                low_ref[:, 2 * HEAD_SIZE : 3 * HEAD_SIZE], low_ref[at, lanes],
                key_row_ref[...], row_ref[:, at], start_ref[:, at],
            )
            top = jnp.max(scores, axis=0, keepdims=True)
            exponent = jnp.exp(scores - top)
            summed = jnp.sum(exponent, axis=0, keepdims=True)
            probability = (exponent * (1.0 / summed)).astype(BF)
            out_t = dot_f32(value_t[...], probability, ((1,), (0,)))
            attended_ref[at, lanes] = out_t.T.astype(BF)
            log_ref[head : head + 1, at] = top + jnp.log(summed)
        part = dot_f32(attended_ref[at, :], out_weight_ref[...], ((1,), (1,)))
        store_block(parts, block, slice(None), part.astype(BF))


def mlp_kernel(slot_ref, *refs):
    rows, grad_ref, weight_ref, hid_ref, d_ref = refs[:5], *refs[5:9]
    back, part = refs[9:14], refs[14:19]
    for block in range(ALL_ROWS // BLOCK):
        at = slice(block * BLOCK, (block + 1) * BLOCK)
        grads = jnp.concatenate([grad_ref[slot_ref[2 * block]], grad_ref[slot_ref[2 * block + 1]]])
        both = dot_f32(block_of(rows, block), weight_ref[:, :768], ((1,), (0,)))
        gate, up = both[:, :384], both[:, 384:]
        sigmoid = jax.nn.sigmoid(gate)
        silu = gate * sigmoid
        hid = (silu * up).astype(BF)
        hid_ref[at, :] = hid
        d_hid = dot_f32(grads, weight_ref[:, 768:], ((1,), (0,)))
        d_gate = (d_hid * up * sigmoid * (1.0 + gate * (1.0 - sigmoid))).astype(BF)
        d_both = jnp.concatenate([d_gate, (d_hid * silu).astype(BF)], axis=1)
        d_ref[at, :] = d_both
        d_rows = dot_f32(d_both, weight_ref[:, :768], ((1,), (1,)))
        store_block(back, block, slice(None), d_rows.astype(BF))
        out_rows = dot_f32(hid, weight_ref[:, 768:], ((1,), (1,)))
        store_block(part, block, slice(None), out_rows.astype(BF))


def split_rows(me, whole, keep_ref, send_ref):
    core = lax.rem(me, 2)
    for slot in range(8):
        at = slice(slot * SHARD, (slot + 1) * SHARD)
        keep_ref[at] = whole[pl.ds(slot_place(me, slot, core), SHARD), :]
        send_ref[at] = whole[pl.ds(slot_place(me, slot, 1 - core), SHARD), :].astype(BF)


def assemble(parts, whole):
    for block in range(ALL_ROWS // BLOCK):
        whole[block * BLOCK : (block + 1) * BLOCK] = block_of(parts, block)


def mlp_grads_kernel(me_ref, slot_ref, *refs):
    grad_ref, hid_ref, d_ref, keep_ref, send_ref, whole, grads, rows = refs[5:]
    assemble(refs[:5], rows)
    for slot in range(TENSOR):
        grads[slot * ROWS : (slot + 1) * ROWS] = grad_ref[slot_ref[slot]]
    for block in range(MODEL_WIDTH // BLOCK):
        at = slice(block * BLOCK, (block + 1) * BLOCK)
        whole[at, :768] = dot_f32(rows[:, at], d_ref[...], ((0,), (0,)))
        whole[at, 768:] = dot_f32(grads[:, at], hid_ref[...], ((0,), (0,)))
    split_rows(me_ref[0], whole, keep_ref, send_ref)


def attn_grads_kernel(me_ref, *refs):
    d_ref, attended_ref, keep_ref, send_ref, whole, rows, back = refs[10:]
    assemble(refs[:5], rows)
    assemble(refs[5:10], back)
    for block in range(MODEL_WIDTH // BLOCK):
        at = slice(block * BLOCK, (block + 1) * BLOCK)
        whole[at, :512] = dot_f32(rows[:, at], d_ref[...], ((0,), (0,)))
        whole[at, 512:] = dot_f32(back[:, at], attended_ref[...], ((0,), (0,)))
    split_rows(me_ref[0], whole, keep_ref, send_ref)


def backward_kernel(*refs):
    back, rows, mlp_parts, refs = refs[:5], refs[5:10], refs[10:15], refs[15:]
    raw_ref, low_ref, log_ref, weight_ref, out_weight_ref, cos_ref, sin_ref = refs[:7]
    gain_ref, norm_gain_ref, key_row_ref, row_ref, start_ref = refs[7:12]
    d_ref, gain_grad_ref, norm_grad_ref, parts = *refs[12:15], refs[15:20]
    d_key, d_value, key_t = refs[20:]
    keys = slice(2 * HEAD_SIZE, 3 * HEAD_SIZE)
    values = slice(3 * HEAD_SIZE, 4 * HEAD_SIZE)
    key_t[...] = low_ref[:, keys].T
    d_key[...] = jnp.zeros_like(d_key)
    d_value[...] = jnp.zeros_like(d_value)

    def through_norm(turned, raw, cosine, sine, gain):
        scaled = turned * cosine + pltpu.roll(turned * sine, HEAD_SIZE // 2, 1)
        inverse = inverse_size(raw)
        weighted = scaled * gain
        mean = jnp.mean(weighted * raw, axis=-1, keepdims=True)
        grad = inverse * weighted - raw * (inverse * inverse * inverse * mean)
        return grad.astype(BF), jnp.sum(scaled * raw * inverse, axis=0, keepdims=True)

    query_gain_grad = jnp.zeros((1, HEAD_SIZE), F32)
    for block in range(ALL_ROWS // BLOCK):
        at = slice(block * BLOCK, (block + 1) * BLOCK)
        d_attended = dot_f32(block_of(back, block), out_weight_ref[...], ((1,), (0,))).astype(BF)
        for head in range(2):
            lanes = slice(head * HEAD_SIZE, (head + 1) * HEAD_SIZE)
            queries = low_ref[at, lanes]
            d_out = d_attended[:, lanes]
            scores = scores_of(
                low_ref[:, keys], queries, key_row_ref[...], row_ref[:, at], start_ref[:, at]
            )
            probability = jnp.exp(scores - log_ref[head : head + 1, at])
            d_prob = dot_f32(low_ref[:, values], d_out, ((1,), (1,)))
            row_dot = jnp.sum(probability * d_prob, axis=0, keepdims=True)
            d_score = (probability * (d_prob - row_dot)).astype(BF)
            d_value[...] += dot_f32(probability.astype(BF), d_out, ((1,), (0,)))
            d_key[...] += dot_f32(d_score, queries, ((1,), (0,)))
            d_query_t = dot_f32(key_t[...], d_score, ((1,), (0,)))
            grad, gain_part = through_norm(
                d_query_t.T * SCORE_SCALE, raw_ref[at, lanes], cos_ref[at, :], sin_ref[at, :],
                gain_ref[0:1, :],
            )
            d_ref[at, lanes] = grad
            query_gain_grad = query_gain_grad + gain_part
    key_gain_grad = jnp.zeros((1, HEAD_SIZE), F32)
    norm_grad = jnp.zeros((1, MODEL_WIDTH), F32)
    for block in range(ALL_ROWS // BLOCK):
        at = slice(block * BLOCK, (block + 1) * BLOCK)
        grad, gain_part = through_norm(
            d_key[at, :] * SCORE_SCALE, raw_ref[at, keys], cos_ref[at, :], sin_ref[at, :],
            gain_ref[1:2, :],
        )
        d_ref[at, keys] = grad
        d_ref[at, values] = d_value[at, :].astype(BF)
        key_gain_grad = key_gain_grad + gain_part
        part = dot_f32(d_ref[at, :], weight_ref[...], ((1,), (1,)))
        normal = block_of(rows, block).astype(F32)
        norm_grad = norm_grad + jnp.sum(part * normal, axis=0, keepdims=True)
        store_block(parts, block, slice(0, MODEL_WIDTH), part.astype(BF))
        store_block(parts, block, slice(MODEL_WIDTH, None), block_of(mlp_parts, block))
    norm_grad_ref[...] = norm_grad / norm_gain_ref[...]
    gain_grad_ref[0:1, :] = query_gain_grad
    gain_grad_ref[1:2, :] = key_gain_grad


def scatter_data(pair, beside=plain):
    keep, other = pair
    both = keep + send(other, TURN_CORE).astype(F32)
    parts, first = [], 0
    for rows in part_rows(SHARD):
        parts.append(both[first : first + rows])
        first += rows
    return ring_scatter(parts, OVER_DATA, beside)


def shape(rows, columns, kind):
    return jax.ShapeDtypeStruct((rows, columns), kind)


def part_shapes(columns):
    return [shape(rows, columns, BF) for rows in part_rows(ROWS)]


def split_shapes(width):
    return [shape(8 * SHARD, width, F32), shape(8 * SHARD, width, BF)]


def pack_kernel(me_ref, rows_ref, *outs):
    me = me_ref[0]
    kind = lax.rem(me, 2) + 2 * (me // 8)
    width = outs[0].shape[1]
    for turn in range(4):
        number = jnp.minimum(jnp.bitwise_xor(kind, turn), 2)
        for choice in range(3):

            @pl.when(number == choice)
            def _(turn=turn, choice=choice):
                outs[turn][...] = rows_ref[:, choice * width : (choice + 1) * width].astype(BF)


def split_low(value):
    high = value.astype(BF)
    return high, (value - high.astype(F32)).astype(BF)


def dot_f32(left, right, dims):
    return lax.dot_general(left, right, (dims, ((), ())), preferred_element_type=F32)


def orthogonal_kernel(paired, turns, first, last, me_ref, *refs):
    kind = lax.rem(me_ref[0], 2) + 2 * (me_ref[0] // 8)
    taken = 5 if first else 1
    parts, outs, current = refs[:taken], refs[taken:-1], refs[-1]
    width = current.shape[1]
    if paired is not None:
        down = lax.broadcasted_iota(jnp.int32, (width, width), 0) < width // 2
        across = lax.broadcasted_iota(jnp.int32, (width, width), 1) < width // 2
        apart = (down != across) & (kind == paired)
    if first:
        at = 0
        for part in parts:
            current[at : at + part.shape[0]] = part[...].astype(F32)
            at += part.shape[0]
        matrix = current[...]
        columns = jnp.sum(matrix * matrix, axis=0, keepdims=True)
        size = jnp.sum(columns, keepdims=True)
        if paired is not None:
            place = lax.broadcasted_iota(jnp.int32, (1, width), 1) < width // 2
            left = jnp.sum(jnp.where(place, columns, 0.0), keepdims=True)
            right = jnp.sum(jnp.where(place, 0.0, columns), keepdims=True)
            size = jnp.where(kind == paired, jnp.where(place, left, right), size)
        current[...] = matrix / (jnp.sqrt(size) + 1e-07)
    else:
        current[...] = parts[0][...]

    def polynomial(high, low):
        cross = dot_f32(high, low, ((0,), (0,)))
        gram = dot_f32(high, high, ((0,), (0,))) + (cross + cross.T)
        if paired is not None:
            gram = jnp.where(apart, 0.0, gram)
        gram_high, gram_low = split_low(gram)
        cross = dot_f32(gram_high, gram_low, ((1,), (0,)))
        square = dot_f32(gram_high, gram_high, ((1,), (0,))) + (cross + cross.T)
        return split_low(NS_B * gram + NS_C * square)

    def moved(value, high, low, poly_high, poly_low):
        change = dot_f32(high, poly_high, ((1,), (0,)))
        change = change + dot_f32(high, poly_low, ((1,), (0,)))
        change = change + dot_f32(low, poly_high, ((1,), (0,)))
        return NS_A * value + change

    def turn(_, carry):
        value = current[...]
        high, low = split_low(value)
        poly_high, poly_low = polynomial(high, low)
        current[...] = moved(value, high, low, poly_high, poly_low)
        return carry

    lax.fori_loop(0, turns - 1 if last else turns, turn, 0)
    if not last:
        outs[0][...] = current[...]
        return
    high, low = split_low(current[...])
    poly_high, poly_low = polynomial(high, low)
    rows = 4 * SHARD
    final = moved(current[:rows], high[:rows], low[:rows], poly_high, poly_low)
    for number in range(4):
        outs[number][...] = final[number * SHARD : (number + 1) * SHARD].astype(BF)


def update_kernel(rates, me_ref, master_ref, *refs):
    turned, out = refs[:4], refs[4]
    me = me_ref[0]
    kind = lax.rem(me, 2) + 2 * (me // 8)
    width = turned[0].shape[1]
    for turn in range(4):
        for number in range(3):

            @pl.when(jnp.bitwise_xor(kind, turn) == number)
            def _(turn=turn, number=number):
                at = slice(number * width, (number + 1) * width)
                out[:, at] = master_ref[:, at] - rates[number] * turned[turn][...].astype(F32)


MUON_TURNS = (TURN_CORE, TURN_FAR, TURN_BOTH)


def muon_quarter(me, renewed, beside=plain):
    packed = pl.pallas_call(
        pack_kernel,
        in_specs=[SCALAR] + whole_specs(1),
        out_specs=whole_specs(4),
        out_shape=[shape(SHARD, renewed.shape[1] // 3, BF)] * 4,
        compiler_params=room(48),
        name="muon_pack",
    )(me, renewed)
    moving = beside(*packed[1:])
    return jnp.concatenate(
        [packed[0]] + [send(block, turn) for block, turn in zip(moving, MUON_TURNS)], axis=0
    )


def muon_turns(me, parts, paired, count, first, last):
    width = parts[0].shape[1]
    flops = 27.0 * count * DATA * SHARD * width * width
    return pl.pallas_call(
        functools.partial(orthogonal_kernel, paired, count, first, last),
        in_specs=[SCALAR] + whole_specs(len(parts)),
        out_specs=whole_specs(4 if last else 1),
        out_shape=[shape(SHARD, width, BF)] * 4 if last else [shape(DATA * SHARD, width, F32)],
        scratch_shapes=[pltpu.VMEM((DATA * SHARD, width), F32)],
        compiler_params=room(48),
        cost_estimate=cost(flops, 2e6),
        name="muon_turns",
    )(me, *parts)


def muon_finish(me, turned, masters, rates):
    back = [turned[0]] + [send(block, turn) for block, turn in zip(turned[1:], MUON_TURNS)]
    return pl.pallas_call(
        lambda *refs: update_kernel(rates, *refs),
        in_specs=[SCALAR] + whole_specs(5),
        out_specs=whole_specs(1)[0],
        out_shape=jax.ShapeDtypeStruct(masters.shape, F32),
        compiler_params=room(48),
        name="muon_update",
    )(me, masters, *back)


GAIN_LINKS = [("tensor", [(i, i ^ turn) for i in range(TENSOR)]) for turn in (1, 2, 4)] + [
    ("dp", [(i, i ^ turn) for i in range(DATA)]) for turn in (1, 2, 4, 8)
]


class Beside:
    def __init__(self, me, parts, gain, late):
        self.me, self.parts, self.gain, self.late = me, list(parts), gain, list(late)
        self.stage = 0

    def gain_step(self):
        self.gain = self.gain + send(self.gain, GAIN_LINKS[self.stage])
        self.stage += 1

    def __call__(self, *payload):
        late = self.late if self.stage == 1 else []
        tied = lax.optimization_barrier((*payload, self.gain, *late, *self.parts))
        payload, rest = tied[: len(payload)], tied[len(payload) :]
        self.gain, rest = rest[0], rest[1:]
        if late:
            self.late, rest = list(rest[: len(late)]), rest[len(late) :]
        self.parts = list(rest)
        if self.stage < NS_ITERS:
            first, last = self.stage == 0, self.stage == NS_ITERS - 1
            self.parts = muon_turns(self.me, self.parts, None, 1, first, last)
        self.gain_step()
        return payload


def local(
    tokens,
    out_grad,
    lengths,
    w_query,
    key_weight,
    value_weight,
    w_output,
    w_gate,
    w_up,
    w_down,
    momentum_query,
    key_momentum_buffer,
    value_momentum_buffer,
    momentum_output,
    momentum_gate,
    momentum_up,
    momentum_down,
    gains,
    gain_first,
    gain_second,
):
    tensor_index = lax.axis_index("tensor")
    data_index = lax.axis_index("dp")
    me = data_index.astype(jnp.int32).reshape(1)
    attn_masters = jnp.concatenate([w_query, key_weight, value_weight, w_output.T], axis=1)
    mlp_masters = jnp.concatenate([w_gate, w_up, w_down.T], axis=1)
    attn_moments = jnp.concatenate(
        [momentum_query, key_momentum_buffer, value_momentum_buffer, momentum_output.T], axis=1
    )
    mlp_moments = jnp.concatenate([momentum_gate, momentum_up, momentum_down.T], axis=1)
    g_attn = gains[:MODEL_WIDTH]
    g_mlp = gains[MODEL_WIDTH : 2 * MODEL_WIDTH]
    query_gain = gains[2 * MODEL_WIDTH : 2 * MODEL_WIDTH + HEAD_SIZE]
    g_key = gains[2 * MODEL_WIDTH + HEAD_SIZE :]
    inputs = tokens.astype(F32)
    normal_rows = ring_gather(root_mean_square_norm(inputs, g_attn).astype(BF), OVER_TENSOR)
    qkv_full, output_full, mlp_weights = gather_data(
        jnp.concatenate([attn_masters, mlp_masters], axis=1).astype(BF), me, (512, 256, 1152)
    )
    slots = [
        lax.rem(tensor_index // 2 + STEPS[s] + 4, 4) * 2 + jnp.bitwise_xor(tensor_index % 2, s % 2)
        for s in range(TENSOR)
    ]
    late_grad, *normal_rows = lax.optimization_barrier((out_grad, *normal_rows))
    in_order = lax.all_gather(late_grad, "tensor", axis=0)
    slot_list = jnp.stack(slots).astype(jnp.int32)
    row_index = jnp.concatenate([slot * ROWS + jnp.arange(ROWS, dtype=jnp.int32) for slot in slots])
    segment, token_position = sequence_layout(lengths[0], row_index)
    half = HEAD_SIZE // 2
    frequency = THETA ** (-jnp.arange(half, dtype=F32) * 2.0 / HEAD_SIZE)
    angles = token_position.astype(F32)[:, None] * frequency[None, :]
    cosine, sine = jnp.cos(angles), jnp.sin(angles)
    cosine = jnp.concatenate([cosine, cosine], axis=1)
    sine = jnp.concatenate([-sine, sine], axis=1)
    head_gains = jnp.stack([query_gain, g_key])
    key_row = row_index[:, None]
    query_row = row_index[None, :]
    query_start = (row_index - token_position)[None, :]
    raw, rotated, attn_low, logsum, *branch_part = pl.pallas_call(
        forward_kernel,
        in_specs=whole_specs(13),
        out_specs=whole_specs(9),
        out_shape=[
            shape(ALL_ROWS, 512, F32),
            shape(ALL_ROWS, 512, BF),
            shape(ALL_ROWS, 256, BF),
            shape(2, ALL_ROWS, F32),
            *part_shapes(MODEL_WIDTH),
        ],
        scratch_shapes=[pltpu.VMEM((HEAD_SIZE, ALL_ROWS), BF)],
        compiler_params=room(48),
        cost_estimate=cost(2.7e9, 12e6),
        name="attention_forward",
    )(
        *normal_rows, qkv_full, output_full, cosine, sine, head_gains,
        key_row, query_row, query_start,
    )
    branch_out = ring_scatter(branch_part, OVER_TENSOR)
    hidden_in = inputs + branch_out
    n_two = ring_gather(root_mean_square_norm(hidden_in, g_mlp).astype(BF), OVER_TENSOR)
    inner_act, d_both, *mlp_parts = pl.pallas_call(
        mlp_kernel,
        in_specs=[SCALAR] + whole_specs(7),
        out_specs=whole_specs(12),
        out_shape=[
            shape(ALL_ROWS, 384, BF),
            shape(ALL_ROWS, 768, BF),
            *part_shapes(MODEL_WIDTH),
            *part_shapes(MODEL_WIDTH),
        ],
        compiler_params=room(48),
        cost_estimate=cost(4.9e9, 12e6),
        name="mlp_both_ways",
    )(slot_list, *n_two, in_order, mlp_weights)
    d_norm_two = ring_scatter(mlp_parts[:5], OVER_TENSOR)
    mlp_grads = pl.pallas_call(
        mlp_grads_kernel,
        in_specs=[SCALAR] * 2 + whole_specs(8),
        out_specs=whole_specs(2),
        out_shape=split_shapes(1152),
        scratch_shapes=[
            pltpu.VMEM((MODEL_WIDTH, 1152), F32),
            pltpu.VMEM((ALL_ROWS, MODEL_WIDTH), BF),
            pltpu.VMEM((ALL_ROWS, MODEL_WIDTH), BF),
        ],
        compiler_params=room(48),
        cost_estimate=cost(2.4e9, 10e6),
        name="mlp_grads",
    )(me, slot_list, *n_two, in_order, inner_act, d_both)
    mlp_reduced = scatter_data(mlp_grads)
    mlp_renewed = MOMENTUM * mlp_moments + mlp_reduced
    mlp_rates = (1.0, 1.0, math.sqrt(MODEL_WIDTH / FF))
    mlp_own = muon_quarter(me, mlp_renewed)
    _, norm_two_back = jax.vjp(root_mean_square_norm, hidden_in, g_mlp)
    d_hidden_in, dg_mlp = norm_two_back(d_norm_two)
    d_residual = out_grad.astype(F32) + d_hidden_in
    residual_rows = ring_gather(d_residual.astype(BF), OVER_TENSOR)
    mlp_own, *residual_rows = lax.optimization_barrier((mlp_own, *residual_rows))
    mlp_below, mlp_above = send(mlp_own, UP_Y), send(mlp_own, DOWN_Y)
    d_qkv, head_gain_grads, dg_attn, *last_parts = pl.pallas_call(
        backward_kernel,
        in_specs=whole_specs(27),
        out_specs=whole_specs(8),
        out_shape=[
            shape(ALL_ROWS, 512, BF),
            shape(2, HEAD_SIZE, F32),
            shape(1, MODEL_WIDTH, F32),
            *part_shapes(2 * MODEL_WIDTH),
        ],
        scratch_shapes=[
            pltpu.VMEM((ALL_ROWS, HEAD_SIZE), F32),
            pltpu.VMEM((ALL_ROWS, HEAD_SIZE), F32),
            pltpu.VMEM((HEAD_SIZE, ALL_ROWS), BF),
        ],
        compiler_params=room(48),
        cost_estimate=cost(4.2e9, 14e6),
        name="attention_backward",
    )(
        *residual_rows, *normal_rows, *mlp_parts[5:], raw, rotated, logsum, qkv_full, output_full,
        cosine, sine, head_gains, g_attn[None, :], key_row, query_row, query_start,
    )
    d_qkv, mlp_below, mlp_above = lax.optimization_barrier((d_qkv, mlp_below, mlp_above))
    attn_grads = pl.pallas_call(
        attn_grads_kernel,
        in_specs=[SCALAR] + whole_specs(12),
        out_specs=whole_specs(2),
        out_shape=split_shapes(768),
        scratch_shapes=[
            pltpu.VMEM((MODEL_WIDTH, 768), F32),
            pltpu.VMEM((ALL_ROWS, MODEL_WIDTH), BF),
            pltpu.VMEM((ALL_ROWS, MODEL_WIDTH), BF),
        ],
        compiler_params=room(48),
        cost_estimate=cost(1.6e9, 10e6),
        name="attention_grads",
    )(me, *normal_rows, *residual_rows, d_qkv, attn_low)
    half = 2 * SHARD
    gain_grad = jnp.concatenate([dg_attn[0], dg_mlp, head_gain_grads[0], head_gain_grads[1]])
    keep, other, low_half, high_half = lax.optimization_barrier(
        (*attn_grads, mlp_below[:half], mlp_above[half:])
    )
    far_halves = [send(low_half, UP_Y), send(high_half, DOWN_Y)]
    turns = Beside(me, [mlp_own, mlp_below, mlp_above] + far_halves, gain_grad, last_parts)
    attn_reduced = scatter_data((keep, other), turns)
    attn_renewed = MOMENTUM * attn_moments + attn_reduced
    (attn_own,) = turns(muon_quarter(me, attn_renewed, turns))
    attn_parts = [attn_own] + ring_spread(attn_own, UP_Y, DOWN_Y, turns)
    mlp_updated = muon_finish(me, turns.parts, mlp_masters, mlp_rates)
    attn_updated = muon_finish(
        me,
        muon_turns(me, attn_parts, 1, NS_ITERS, True, True),
        attn_masters,
        (1.0, 1.0, math.sqrt(MODEL_WIDTH / (QUERY_HEADS * HEAD_SIZE // 16))),
    )
    both = ring_scatter(turns.late, OVER_TENSOR)
    d_norm_one, mlp_out = both[:, :MODEL_WIDTH], both[:, MODEL_WIDTH:]
    result = (hidden_in + mlp_out).astype(BF)
    _, norm_one_back = jax.vjp(root_mean_square_norm, inputs, g_attn)
    d_inputs, _ = norm_one_back(d_norm_one)
    tokens_grad = d_residual + d_inputs
    while turns.stage < len(GAIN_LINKS):
        turns.gain_step()
    gain_grad = turns.gain
    renewed_first = BETA_ONE * gain_first + (1.0 - BETA_ONE) * gain_grad
    renewed_second = BETA_TWO * gain_second + (1.0 - BETA_TWO) * gain_grad * gain_grad
    corrected_first = renewed_first / (1.0 - BETA_ONE**ADAM_STEP)
    corrected_second = renewed_second / (1.0 - BETA_TWO**ADAM_STEP)
    updated_gains = gains - GAIN_RATE * corrected_first / (jnp.sqrt(corrected_second) + ADAM_EPS)

    def unpack(attn, mlp):
        return (
            attn[:, :256],
            attn[:, 256:384],
            attn[:, 384:512],
            attn[:, 512:].T,
            mlp[:, :384],
            mlp[:, 384:768],
            mlp[:, 768:].T,
        )

    return (
        result,
        tokens_grad,
        *unpack(attn_reduced, mlp_reduced),
        *unpack(attn_renewed, mlp_renewed),
        *unpack(attn_updated, mlp_updated),
        gain_grad,
        renewed_first,
        renewed_second,
        updated_gains,
    )


def solution(mesh):
    placed = (
        P(("dp", "tensor"), None),
        P(("dp", "tensor"), None),
        P("dp", None),
        P("dp", "tensor"),
        P("dp", "tensor"),
        P("dp", "tensor"),
        P("tensor", "dp"),
        P("dp", "tensor"),
        P("dp", "tensor"),
        P("tensor", "dp"),
        P("dp", "tensor"),
        P("dp", "tensor"),
        P("dp", "tensor"),
        P("tensor", "dp"),
        P("dp", "tensor"),
        P("dp", "tensor"),
        P("tensor", "dp"),
        P(),
        P(),
        P(),
    )
    return jax.shard_map(
        local,
        mesh=mesh,
        in_specs=placed,
        out_specs=(
            P(("dp", "tensor"), None),
            P(("dp", "tensor"), None),
            P("dp", "tensor"),
            P("dp", "tensor"),
            P("dp", "tensor"),
            P("tensor", "dp"),
            P("dp", "tensor"),
            P("dp", "tensor"),
            P("tensor", "dp"),
            P("dp", "tensor"),
            P("dp", "tensor"),
            P("dp", "tensor"),
            P("tensor", "dp"),
            P("dp", "tensor"),
            P("dp", "tensor"),
            P("tensor", "dp"),
            P("dp", "tensor"),
            P("dp", "tensor"),
            P("dp", "tensor"),
            P("tensor", "dp"),
            P("dp", "tensor"),
            P("dp", "tensor"),
            P("tensor", "dp"),
            P(),
            P(),
            P(),
            P(),
        ),
        check_vma=False,
    )
```
